32 devices in a mesh: groups: 2 (over x), gx: 8 (over z, y), gy: 2 (over core).
Axes of the slice: x: 2, y: 2, z: 4, core: 2. Of those that a mesh axis runs over, the one named last changes fastest.
Arguments:
- states: bfloat16 [2048, 16384], P('groups', ('gy', 'gx')), parts along dimension 0
- norm_gain: bfloat16 [16384], P(('gy', 'gx')), may hold values from 0.099609375 to 1.8984375
- w_query: bfloat16 [16384, 8192], P('gy', 'gx'), may hold values from -0.046875 to 0.046875
- keyvalue_weight: bfloat16 [16384, 1024], P('gy', 'gx'), may hold values from -0.046875 to 0.046875
- w_output: bfloat16 [8192, 2, 8, 1024], P('gx', 'gy'), may hold values from -0.25 to 0.25
- key_cache: bfloat16 [2048, 4, 64, 128], P(('groups', 'gy', 'gx')), parts along dimension 0
- cached_value_rows: bfloat16 [2048, 4, 64, 128], P(('groups', 'gy', 'gx')), parts along dimension 0, may hold values from -6 to 6
- lengths: int32 [2048], P(('groups', 'gy', 'gx')), parts along dimension 0, may hold values from 1 to 64, as said below
Outputs:
- layer_out: bfloat16 [2048, 16384], P('groups', ('gy', 'gx')), parts along dimension 0
The draws below stay inside these ranges and needn't reach their ends.
There are 2 independent parts, one for each index of `groups`. The reference program is written for one: setup_inputs(seed, part) draws one part's arguments, and reference() takes and returns one part's arrays. A program takes and returns all parts, laid end to end along the dimension named above; an argument that names none is the same for every part. Nothing has to cross between parts.
Inputs may be any that keep to these rules, and one draw needn't show every extreme that they name: `lengths`: the largest, 64, is reached in every draw.
All inputs are finite; a program needn't handle non-finite values.
Results may differ from the reference program's by a relative error of at most 0.017.
Values may be sent and summed in bfloat16 or wider, within the bound.
A program may use at most 192 MiB of HBM per device.

```python
import math
import jax
import jax.numpy as jnp
from jax import lax

MODEL_WIDTH = 16384
HEAD_SIZE = 128
HQ = 64
KEYVALUE_HEADS = 4
REQUEST_ROWS = 1024
CONTEXT_LENGTH = 64
N_GX = 8
N_GY = 2


def draw_states(key, part):
    key = jax.random.fold_in(key, 11)
    key_base, key_rows, key_cols = jax.random.split(key, 3)
    base_draw = jnp.clip(jax.random.normal(key_base, (REQUEST_ROWS, MODEL_WIDTH), jnp.float32), -3.0, 3.0)
    rise_factor = 3.0
    row_scale = jnp.exp(jax.random.uniform(key_rows, (REQUEST_ROWS, 1), jnp.float32, 0.0, math.log(10.0)))
    col_scale = jnp.exp(jax.random.uniform(key_cols, (1, MODEL_WIDTH), jnp.float32, 0.0, math.log(10.0)))
    ramp = jnp.exp(math.log(rise_factor) * jnp.arange(MODEL_WIDTH, dtype=jnp.float32)[None, :] / MODEL_WIDTH)
    return (0.05 * base_draw * row_scale * col_scale * ramp).astype(jnp.bfloat16)


def draw_key_cache(key, part):
    key = jax.random.fold_in(key, 23)
    primary_key = jax.random.fold_in(key, 0)
    primary_sample = jax.random.normal(primary_key, (REQUEST_ROWS, KEYVALUE_HEADS, CONTEXT_LENGTH, HEAD_SIZE), jnp.float32)
    return primary_sample.astype(jnp.bfloat16)


def draw_lengths(key, part):
    key = jax.random.fold_in(key, 37)
    drawn = jax.random.randint(key, (REQUEST_ROWS,), 1, CONTEXT_LENGTH + 1)
    full_rows = jnp.arange(REQUEST_ROWS) % 32 == 0
    return jnp.where(full_rows, CONTEXT_LENGTH, drawn).astype(jnp.int32)


def raised(values, key, source, target, blocks, factor):
    def block_of(axis_at):
        return (jnp.arange(values.shape[axis_at]) // (values.shape[axis_at] // blocks)).reshape((-1,) + (1,) * (values.ndim - 1 - axis_at))

    near = jax.random.permutation(key, blocks)[block_of(target)]
    other_side = (block_of(target) + blocks // 2) % blocks
    return jnp.where((block_of(source) == near) | (block_of(source) == other_side), factor * values, values)


def block_levels(own_key, shape, pieces, least, high):
    loudness = 1.0
    for dim, parts in pieces:
        heights = jax.random.uniform(jax.random.fold_in(jax.random.fold_in(own_key, 6), dim), (parts,), jnp.float32, least / len(pieces), high / len(pieces))
        loudness = loudness * jnp.repeat(jnp.exp(heights), shape[dim] // parts).reshape((-1,) + (1,) * (len(shape) - 1 - dim))
    return loudness


def scatter_about(rng, extent, width, most, cuts=(), kind=jnp.bfloat16):
    result = width * jax.random.normal(rng, extent, jnp.float32)
    if cuts:
        result = result * block_levels(rng, extent, cuts, -0.22, 0.18)
    return jnp.clip(result, -most, most).astype(kind)


def bell_draw_with(rng, dims, deviation, most, cuts, heavy, kind=jnp.bfloat16):
    result = deviation * jax.random.normal(rng, dims, jnp.float32)
    if cuts:
        result = result * block_levels(rng, dims, cuts, -0.22, 0.18)
    return jnp.clip(raised(result, jax.random.fold_in(rng, 3), *heavy), -most, most).astype(kind)


def setup_inputs(seed: int = 0, part: int = 0) -> dict:
    key_list = jax.random.split(jax.random.key(seed), 9)
    part_splits = jax.random.split(jax.random.fold_in(key_list[8], part), 9)
    return {
        "states": draw_states(jax.random.fold_in(jax.random.fold_in(key_list[8], part), 71), part),
        "norm_gain": jnp.clip(1.0 + 0.18 * jax.random.normal(key_list[1], (MODEL_WIDTH,), jnp.float32), 0.099609375, 1.8984375).astype(jnp.bfloat16),
        "w_query": scatter_about(key_list[2], (MODEL_WIDTH, HQ * HEAD_SIZE), MODEL_WIDTH ** -0.5, 0.046875, ((0, 2), (1, 8))),
        "keyvalue_weight": scatter_about(key_list[3], (MODEL_WIDTH, 2 * KEYVALUE_HEADS * HEAD_SIZE), MODEL_WIDTH ** -0.5, 0.046875, ((0, 2), (1, 8))),
        "w_output": bell_draw_with(key_list[4], (HQ * HEAD_SIZE, N_GY, N_GX, MODEL_WIDTH // (N_GX * N_GY)), (HQ * HEAD_SIZE // 8) ** -0.5, 0.25, ((0, 8), (1, 2)), (0, 2, 8, 2.0)),
        "key_cache": draw_key_cache(jax.random.fold_in(jax.random.fold_in(key_list[8], part), 71), part),
        "cached_value_rows": scatter_about(part_splits[6], (REQUEST_ROWS, KEYVALUE_HEADS, CONTEXT_LENGTH, HEAD_SIZE), 1.0, 6.0, ((0, 16),)),
        "lengths": draw_lengths(jax.random.fold_in(jax.random.fold_in(key_list[8], part), 71), part),
    }


epsilon = 1e-05
rope_base = 500000.0

def rotate(vectors, positions):
    middle = vectors.shape[-1] // 2
    frequency = rope_base ** (-jnp.arange(middle, dtype=jnp.float32) * 2.0 / vectors.shape[-1])
    angles = positions.astype(jnp.float32)[:, None] * frequency[None, :]
    cosine = jnp.cos(angles)[:, None, :]
    sine_part = jnp.sin(angles)[:, None, :]
    leading = vectors[..., :middle]
    trailing = vectors[..., middle:]
    return jnp.concatenate([leading * cosine - trailing * sine_part, trailing * cosine + leading * sine_part], axis=-1)

def attend(queries, new_keys, new_values, key_cache, cached_value_rows, lengths):
    row_count, kv_heads, context, head_dim = key_cache.shape
    heads = queries.shape[1] // head_dim
    per_group = heads // kv_heads
    query_rot = rotate(queries.astype(jnp.float32).reshape(row_count, heads, head_dim), lengths).astype(jnp.bfloat16)
    key_rot = rotate(new_keys.astype(jnp.float32).reshape(row_count, kv_heads, head_dim), lengths).astype(jnp.bfloat16)
    query_grp = query_rot.reshape(row_count, kv_heads, per_group, head_dim).astype(jnp.float32)
    scaling = 1.0 / math.sqrt(head_dim)
    cached = jnp.einsum('rgjd,rgcd->rgjc', query_grp, key_cache.astype(jnp.float32)) * scaling
    own_score = jnp.einsum('rgjd,rgd->rgj', query_grp, key_rot.astype(jnp.float32)) * scaling
    is_live = (jnp.arange(context)[None, :] < lengths[:, None])[:, None, None, :]
    cached = jnp.where(is_live, cached, -jnp.inf)
    peak_score = jnp.maximum(lax.optimization_barrier(jnp.max(cached, axis=-1)), own_score)
    weights = jnp.where(is_live, jnp.exp(cached - peak_score[..., None]), 0.0)
    own_weight = jnp.exp(own_score - peak_score)
    total = lax.optimization_barrier(jnp.sum(weights, axis=-1)) + own_weight
    probs = lax.optimization_barrier(weights.astype(jnp.bfloat16)).astype(jnp.float32)
    own_prob = lax.optimization_barrier(own_weight.astype(jnp.bfloat16)).astype(jnp.float32)
    mixed = jnp.einsum('rgjc,rgcd->rgjd', probs, cached_value_rows.astype(jnp.float32))
    mixed = mixed + own_prob[..., None] * new_values.astype(jnp.float32).reshape(row_count, kv_heads, 1, head_dim)
    return (mixed / total[..., None]).astype(jnp.bfloat16).reshape(row_count, heads * head_dim)

def reference(states, norm_gain, w_query, keyvalue_weight, w_output, key_cache, cached_value_rows, lengths):
    states_f = states.astype(jnp.float32)
    norm_scale = lax.rsqrt(lax.optimization_barrier(jnp.mean(states_f * states_f, axis=1, keepdims=True)) + epsilon)
    normed = (states_f * norm_scale * norm_gain.astype(jnp.float32)[None, :]).astype(jnp.bfloat16)
    queries = jnp.dot(normed, w_query, preferred_element_type=jnp.float32).astype(jnp.bfloat16)
    keyvals = jnp.dot(normed, keyvalue_weight, preferred_element_type=jnp.float32).astype(jnp.bfloat16)
    key_span_width = KEYVALUE_HEADS * HEAD_SIZE
    attended = attend(queries, keyvals[:, :key_span_width], keyvals[:, key_span_width:], key_cache, cached_value_rows, lengths)
    block_width = HQ * HEAD_SIZE // N_GX
    blocks = jnp.moveaxis(attended.reshape(REQUEST_ROWS, N_GX, block_width), 1, 0)
    weight_blocks = w_output.reshape(N_GX, block_width, MODEL_WIDTH)

    def add_block(running_sum, pair):
        block, weight_rows = pair
        partial_value = jnp.dot(block, weight_rows, preferred_element_type=jnp.float32)
        partial_value = lax.optimization_barrier(partial_value.astype(jnp.bfloat16)).astype(jnp.float32)
        return (running_sum + partial_value, None)
    summed, _ = lax.scan(add_block, jnp.zeros((REQUEST_ROWS, MODEL_WIDTH), jnp.float32), (blocks, weight_blocks))
    return (states_f + summed).astype(jnp.bfloat16)
```

```python
import math

import jax
import jax.numpy as jnp
from jax import lax
from jax.sharding import PartitionSpec as P

MODEL_WIDTH = 16384


epsilon = 1e-05
rope_base = 500000.0


def rotate(vectors, positions):
    middle = vectors.shape[-1] // 2
    frequency = rope_base ** (-jnp.arange(middle, dtype=jnp.float32) * 2.0 / vectors.shape[-1])
    angles = positions.astype(jnp.float32)[:, None] * frequency[None, :]
    cosine = jnp.cos(angles)[:, None, :]
    sine_part = jnp.sin(angles)[:, None, :]
    leading = vectors[..., :middle]
    trailing = vectors[..., middle:]
    return jnp.concatenate(
        [leading * cosine - trailing * sine_part, trailing * cosine + leading * sine_part], axis=-1
    )


def attend(queries, new_keys, new_values, key_cache, cached_value_rows, lengths):
    row_count, kv_heads, context, head_dim = key_cache.shape
    heads = queries.shape[1] // head_dim
    per_group = heads // kv_heads
    query_rot = rotate(
        queries.astype(jnp.float32).reshape(row_count, heads, head_dim), lengths
    ).astype(jnp.bfloat16)
    key_rot = rotate(
        new_keys.astype(jnp.float32).reshape(row_count, kv_heads, head_dim), lengths
    ).astype(jnp.bfloat16)
    query_grp = query_rot.reshape(row_count, kv_heads, per_group, head_dim)
    scaling = 1.0 / math.sqrt(head_dim)
    cached = (
        jnp.einsum("rgjd,rgcd->rgjc", query_grp, key_cache, preferred_element_type=jnp.float32)
        * scaling
    )
    own_score = (
        jnp.einsum("rgjd,rgd->rgj", query_grp, key_rot, preferred_element_type=jnp.float32)
        * scaling
    )
    is_live = (jnp.arange(context)[None, :] < lengths[:, None])[:, None, None, :]
    cached = jnp.where(is_live, cached, -jnp.inf)
    peak_score = jnp.maximum(jnp.max(cached, axis=-1), own_score)
    weights = jnp.where(is_live, jnp.exp(cached - peak_score[..., None]), 0.0)
    own_weight = jnp.exp(own_score - peak_score)
    total = jnp.sum(weights, axis=-1) + own_weight
    own_prob = lax.optimization_barrier(own_weight.astype(jnp.bfloat16)).astype(jnp.float32)
    mixed = jnp.einsum(
        "rgjc,rgcd->rgjd",
        weights.astype(jnp.bfloat16),
        cached_value_rows,
        preferred_element_type=jnp.float32,
    )
    mixed = mixed + own_prob[..., None] * new_values.astype(jnp.float32).reshape(
        row_count, kv_heads, 1, head_dim
    )
    return (mixed / total[..., None]).astype(jnp.bfloat16).reshape(row_count, heads * head_dim)


def ring_order(size):
    if size == 8:
        return [0, 2, 4, 6, 7, 5, 3, 1]
    return list(range(size))


def shards(
    states, norm_gain, w_query, keyvalue_weight, w_output, key_cache, cached_value_rows, lengths
):
    size = lax.axis_size("gx")
    me = lax.axis_index("gx")
    core = lax.axis_index("gy")
    order = ring_order(size)
    order_arr = jnp.array(order, jnp.int32)
    place_arr = jnp.array([order.index(i) for i in range(size)], jnp.int32)
    place = place_arr[me]
    hops = {1: [(order[i], order[(i + 1) % size]) for i in range(size)],
            -1: [(order[(i + 1) % size], order[i]) for i in range(size)]}
    long_way = size // 2
    reach = {(1, 0): long_way, (-1, 0): size - 1 - long_way,
             (1, 1): size - 1 - long_way, (-1, 1): long_way}
    chains = list(reach)

    def at_place(offset):
        return order_arr[lax.rem(place + offset + size, size)]

    row_count, width = states.shape
    half_rows = row_count // 2
    other = 1 - core

    def half_of(array, half):
        return lax.dynamic_slice_in_dim(
            array, jnp.where(half == 0, other, core) * half_rows, half_rows, 0
        )

    state_halves = [half_of(states, 0), half_of(states, 1)]

    states_f = states.astype(jnp.float32)
    gain_all = jnp.zeros((2 * size * width,), jnp.float32)
    gain_all = lax.dynamic_update_slice(
        gain_all, norm_gain.astype(jnp.float32), ((core * size + me) * width,)
    )
    both = lax.psum(
        jnp.concatenate([jnp.sum(states_f * states_f, axis=1), gain_all]), ("gx", "gy")
    )
    norm_scale = lax.rsqrt(both[:row_count] / MODEL_WIDTH + epsilon)
    gain_mine = lax.dynamic_slice_in_dim(both[row_count:], core * size * width, size * width, 0)
    scale_halves = [half_of(norm_scale, 0), half_of(norm_scale, 1)]

    def project(raw, half, owner):
        gain = lax.dynamic_slice_in_dim(gain_mine, owner * width, width, 0)
        normed = (
            raw.astype(jnp.float32) * scale_halves[half][:, None] * gain[None, :]
        ).astype(jnp.bfloat16)
        wq = lax.dynamic_slice_in_dim(w_query, owner * width, width, 0)
        wkv = lax.dynamic_slice_in_dim(keyvalue_weight, owner * width, width, 0)
        return (
            jnp.dot(normed, wq, preferred_element_type=jnp.float32),
            jnp.dot(normed, wkv, preferred_element_type=jnp.float32),
        )

    held = {chain: state_halves[chain[1]] for chain in chains}
    sums = [None, None]

    def add_to(half, pair):
        old = sums[half]
        sums[half] = pair if old is None else (old[0] + pair[0], old[1] + pair[1])

    output_cols = w_output.reshape(w_output.shape[0], size, w_output.shape[3])
    out_blocks = jnp.transpose(output_cols, (1, 0, 2))
    for step in range(1, long_way + 1):
        arrived = {}
        for chain in chains:
            if step <= reach[chain]:
                arrived[chain] = lax.ppermute(held[chain], "gx", hops[chain[0]])
        if step == 1:
            for half in (0, 1):
                add_to(half, project(state_halves[half], half, me))
        if step == 2:
            (out_blocks, last) = lax.optimization_barrier((out_blocks, arrived[chains[0]]))
            arrived[chains[0]] = last
        for chain, raw in arrived.items():
            add_to(chain[1], project(raw, chain[1], at_place(-chain[0] * step)))
        held.update(arrived)

    joined = [jnp.concatenate([q, kv], axis=1).astype(jnp.bfloat16) for q, kv in sums]
    pair = [(0, 1), (1, 0)]
    from_other = lax.ppermute(joined[0], "gy", pair)
    mine = (joined[1].astype(jnp.float32) + from_other.astype(jnp.float32)).astype(jnp.bfloat16)

    query_width = w_query.shape[1]
    rows_here = half_rows // size
    spread = lax.all_to_all(
        mine.reshape(size, rows_here, mine.shape[1]), "gx", split_axis=0, concat_axis=0, tiled=True
    )
    spread = jnp.transpose(spread, (1, 0, 2))
    queries = spread[:, :, :query_width].reshape(rows_here, -1)
    keyvals = spread[:, :, query_width:].reshape(rows_here, -1)
    key_span_width = keyvals.shape[1] // 2
    attended = attend(
        queries,
        keyvals[:, :key_span_width],
        keyvals[:, key_span_width:],
        key_cache,
        cached_value_rows,
        lengths,
    )
    own_rows = lax.all_to_all(attended, "gx", split_axis=1, concat_axis=0, tiled=True)
    other_rows = lax.ppermute(own_rows, "gy", pair)
    head_rows = [other_rows, own_rows]

    def term(half, dest):
        block = lax.dynamic_index_in_dim(out_blocks, dest, 0, keepdims=False)
        return jnp.dot(head_rows[half], block, preferred_element_type=jnp.float32)

    moving = {}
    for step in range(long_way, 0, -1):
        for chain in chains[2:] + chains[:2]:
            if step <= reach[chain]:
                value = term(chain[1], at_place(chain[0] * step))
                if chain in moving:
                    value = value + moving[chain].astype(jnp.float32)
                moving[chain] = lax.ppermute(value.astype(jnp.bfloat16), "gx", hops[chain[0]])
    halves = []
    for half in (0, 1):
        total = state_halves[half].astype(jnp.float32) + term(half, me)
        for chain in chains:
            if chain[1] == half and chain in moving:
                total = total + moving[chain].astype(jnp.float32)
        halves.append(total.astype(jnp.bfloat16))
    out = jnp.zeros((row_count, width), jnp.bfloat16)
    out = lax.dynamic_update_slice(out, halves[0], (other * half_rows, 0))
    return lax.dynamic_update_slice(out, halves[1], (core * half_rows, 0))


def solution(mesh):
    return jax.shard_map(
        shards,
        mesh=mesh,
        in_specs=(
            P("groups", ("gy", "gx")),
            P(("gy", "gx")),
            P("gy", "gx"),
            P("gy", "gx"),
            P("gx", "gy", None, None),
            P(("groups", "gy", "gx"), None, None, None),
            P(("groups", "gy", "gx"), None, None, None),
            P(("groups", "gy", "gx")),
        ),
        out_specs=P("groups", ("gy", "gx")),
        check_vma=False,
    )
```

```python
import math

import jax
import jax.numpy as jnp
from jax import lax
from jax.sharding import PartitionSpec as P

MODEL_WIDTH = 16384


epsilon = 1e-05
rope_base = 500000.0


def rotate(vectors, positions):
    middle = vectors.shape[-1] // 2
    frequency = rope_base ** (-jnp.arange(middle, dtype=jnp.float32) * 2.0 / vectors.shape[-1])
    angles = positions.astype(jnp.float32)[:, None] * frequency[None, :]
    cosine = jnp.cos(angles)[:, None, :]
    sine_part = jnp.sin(angles)[:, None, :]
    leading = vectors[..., :middle]
    trailing = vectors[..., middle:]
    return jnp.concatenate(
        [leading * cosine - trailing * sine_part, trailing * cosine + leading * sine_part], axis=-1
    )


def attend(queries, new_keys, new_values, key_cache, cached_value_rows, lengths):
    row_count, kv_heads, context, head_dim = key_cache.shape
    heads = queries.shape[1] // head_dim
    per_group = heads // kv_heads
    query_rot = rotate(
        queries.astype(jnp.float32).reshape(row_count, heads, head_dim), lengths
    ).astype(jnp.bfloat16)
    key_rot = rotate(
        new_keys.astype(jnp.float32).reshape(row_count, kv_heads, head_dim), lengths
    ).astype(jnp.bfloat16)
    query_grp = query_rot.reshape(row_count, kv_heads, per_group, head_dim)
    scaling = 1.0 / math.sqrt(head_dim)
    cached = (
        jnp.einsum("rgjd,rgcd->rgjc", query_grp, key_cache, preferred_element_type=jnp.float32)
        * scaling
    )
    own_score = (
        jnp.einsum("rgjd,rgd->rgj", query_grp, key_rot, preferred_element_type=jnp.float32)
        * scaling
    )
    is_live = (jnp.arange(context)[None, :] < lengths[:, None])[:, None, None, :]
    cached = jnp.where(is_live, cached, -jnp.inf)
    peak_score = jnp.maximum(jnp.max(cached, axis=-1), own_score)
    weights = jnp.where(is_live, jnp.exp(cached - peak_score[..., None]), 0.0)
    own_weight = jnp.exp(own_score - peak_score)
    total = jnp.sum(weights, axis=-1) + own_weight
    own_prob = lax.optimization_barrier(own_weight.astype(jnp.bfloat16)).astype(jnp.float32)
    mixed = jnp.einsum(
        "rgjc,rgcd->rgjd",
        weights.astype(jnp.bfloat16),
        cached_value_rows,
        preferred_element_type=jnp.float32,
    )
    mixed = mixed + own_prob[..., None] * new_values.astype(jnp.float32).reshape(
        row_count, kv_heads, 1, head_dim
    )
    return (mixed / total[..., None]).astype(jnp.bfloat16).reshape(row_count, heads * head_dim)


def ring_order(size):
    if size == 8:
        return [0, 2, 4, 6, 7, 5, 3, 1]
    return list(range(size))


def shards(
    states, norm_gain, w_query, keyvalue_weight, w_output, key_cache, cached_value_rows, lengths
):
    size = lax.axis_size("gx")
    me = lax.axis_index("gx")
    core = lax.axis_index("gy")
    order = ring_order(size)
    order_arr = jnp.array(order, jnp.int32)
    place_arr = jnp.array([order.index(i) for i in range(size)], jnp.int32)
    place = place_arr[me]
    hops = {1: [(order[i], order[(i + 1) % size]) for i in range(size)],
            -1: [(order[(i + 1) % size], order[i]) for i in range(size)]}
    long_way = size // 2
    reach = {(1, 0): long_way, (-1, 0): size - 1 - long_way,
             (1, 1): size - 1 - long_way, (-1, 1): long_way}
    chains = list(reach)

    def at_place(offset):
        return order_arr[lax.rem(place + offset + size, size)]

    row_count, width = states.shape
    half_rows = row_count // 2
    other = 1 - core

    def half_of(array, half):
        return lax.dynamic_slice_in_dim(
            array, jnp.where(half == 0, other, core) * half_rows, half_rows, 0
        )

    state_halves = [half_of(states, 0), half_of(states, 1)]

    states_f = states.astype(jnp.float32)
    gain_all = lax.dynamic_update_slice(
        jnp.zeros((size * width,), jnp.float32), norm_gain.astype(jnp.float32), (me * width,)
    )
    both = jnp.concatenate([jnp.sum(states_f * states_f, axis=1), gain_all])
    if size & (size - 1) == 0:
        stride = 1
        while stride < size:
            both = both + lax.ppermute(both, "gx", [(i, i ^ stride) for i in range(size)])
            stride *= 2
    else:
        both = lax.psum(both, "gx")
    squares = both[:row_count]
    squares = squares + lax.ppermute(squares, "gy", [(0, 1), (1, 0)])
    norm_scale = lax.rsqrt(squares / MODEL_WIDTH + epsilon)
    gain_mine = both[row_count:]
    scale_halves = [half_of(norm_scale, 0), half_of(norm_scale, 1)]

    def project(raw, half, owner):
        gain = lax.dynamic_slice_in_dim(gain_mine, owner * width, width, 0)
        normed = (
            raw.astype(jnp.float32) * scale_halves[half][:, None] * gain[None, :]
        ).astype(jnp.bfloat16)
        wq = lax.dynamic_slice_in_dim(w_query, owner * width, width, 0)
        wkv = lax.dynamic_slice_in_dim(keyvalue_weight, owner * width, width, 0)
        return (
            jnp.dot(normed, wq, preferred_element_type=jnp.float32),
            jnp.dot(normed, wkv, preferred_element_type=jnp.float32),
        )

    held = {chain: state_halves[chain[1]] for chain in chains}
    sums = [None, None]

    def add_to(half, pair):
        old = sums[half]
        sums[half] = pair if old is None else (old[0] + pair[0], old[1] + pair[1])

    out_blocks = {}

    def load_block(offset, after):
        weight, after = lax.optimization_barrier((w_output, after))
        block = lax.dynamic_index_in_dim(weight[:, 0], at_place(offset), 1, keepdims=False)
        block, after = lax.optimization_barrier((block, after))
        out_blocks[offset % size] = block
        return after

    offsets = list(range(size))
    per_step = -(-size // long_way)
    for step in range(1, long_way + 1):
        arrived = {}
        for chain in chains:
            if step <= reach[chain]:
                arrived[chain] = lax.ppermute(held[chain], "gx", hops[chain[0]])
        if step == 1:
            for half in (0, 1):
                add_to(half, project(state_halves[half], half, me))
        for offset in offsets[(step - 1) * per_step : step * per_step]:
            held_first = chains[0] if chains[0] in arrived else chains[1]
            arrived[held_first] = load_block(offset, arrived[held_first])
        for chain, raw in arrived.items():
            add_to(chain[1], project(raw, chain[1], at_place(-chain[0] * step)))
        held.update(arrived)

    joined = [jnp.concatenate([q, kv], axis=1).astype(jnp.bfloat16) for q, kv in sums]
    pair = [(0, 1), (1, 0)]
    from_other = lax.ppermute(joined[0], "gy", pair)
    mine = (joined[1].astype(jnp.float32) + from_other.astype(jnp.float32)).astype(jnp.bfloat16)

    query_width = w_query.shape[1]
    rows_here = half_rows // size
    spread = lax.all_to_all(
        mine.reshape(size, rows_here, mine.shape[1]), "gx", split_axis=0, concat_axis=0, tiled=True
    )
    spread = jnp.transpose(spread, (1, 0, 2))
    queries = spread[:, :, :query_width].reshape(rows_here, -1)
    keyvals = spread[:, :, query_width:].reshape(rows_here, -1)
    key_span_width = keyvals.shape[1] // 2
    attended = attend(
        queries,
        keyvals[:, :key_span_width],
        keyvals[:, key_span_width:],
        key_cache,
        cached_value_rows,
        lengths,
    )
    own_rows = lax.all_to_all(attended, "gx", split_axis=1, concat_axis=0, tiled=True)
    other_rows = lax.ppermute(own_rows, "gy", pair)
    head_rows = [other_rows, own_rows]

    def term(half, dest):
        return jnp.dot(
            head_rows[half], out_blocks[dest % size], preferred_element_type=jnp.float32
        )

    moving = {}
    for step in range(long_way, 0, -1):
        for chain in chains[2:] + chains[:2]:
            if step <= reach[chain]:
                value = term(chain[1], chain[0] * step)
                if chain in moving:
                    value = value + moving[chain].astype(jnp.float32)
                moving[chain] = lax.ppermute(value.astype(jnp.bfloat16), "gx", hops[chain[0]])
    halves = []
    for half in (0, 1):
        total = state_halves[half].astype(jnp.float32) + term(half, 0)
        for chain in chains:
            if chain[1] == half and chain in moving:
                total = total + moving[chain].astype(jnp.float32)
        halves.append(total.astype(jnp.bfloat16))
    out = jnp.zeros((row_count, width), jnp.bfloat16)
    out = lax.dynamic_update_slice(out, halves[0], (other * half_rows, 0))
    return lax.dynamic_update_slice(out, halves[1], (core * half_rows, 0))


def solution(mesh):
    return jax.shard_map(
        shards,
        mesh=mesh,
        in_specs=(
            P("groups", ("gy", "gx")),
            P(("gy", "gx")),
            P("gy", "gx"),
            P("gy", "gx"),
            P("gx", "gy", None, None),
            P(("groups", "gy", "gx"), None, None, None),
            P(("groups", "gy", "gx"), None, None, None),
            P(("groups", "gy", "gx")),
        ),
        out_specs=P("groups", ("gy", "gx")),
        check_vma=False,
    )
```

```python
import math

import jax
import jax.numpy as jnp
from jax import lax
from jax.sharding import PartitionSpec as P

MODEL_WIDTH = 16384


epsilon = 1e-05
rope_base = 500000.0


def rotate(vectors, positions):
    middle = vectors.shape[-1] // 2
    frequency = rope_base ** (-jnp.arange(middle, dtype=jnp.float32) * 2.0 / vectors.shape[-1])
    angles = positions.astype(jnp.float32)[:, None] * frequency[None, :]
    cosine = jnp.cos(angles)[:, None, :]
    sine_part = jnp.sin(angles)[:, None, :]
    leading = vectors[..., :middle]
    trailing = vectors[..., middle:]
    return jnp.concatenate(
        [leading * cosine - trailing * sine_part, trailing * cosine + leading * sine_part], axis=-1
    )


def attend(queries, new_keys, new_values, key_cache, cached_value_rows, lengths):
    row_count, kv_heads, context, head_dim = key_cache.shape
    heads = queries.shape[1] // head_dim
    per_group = heads // kv_heads
    query_rot = rotate(
        queries.astype(jnp.float32).reshape(row_count, heads, head_dim), lengths
    ).astype(jnp.bfloat16)
    key_rot = rotate(
        new_keys.astype(jnp.float32).reshape(row_count, kv_heads, head_dim), lengths
    ).astype(jnp.bfloat16)
    query_grp = query_rot.reshape(row_count, kv_heads, per_group, head_dim)
    scaling = 1.0 / math.sqrt(head_dim)
    cached = (
        jnp.einsum("rgjd,rgcd->rgjc", query_grp, key_cache, preferred_element_type=jnp.float32)
        * scaling
    )
    own_score = (
        jnp.einsum("rgjd,rgd->rgj", query_grp, key_rot, preferred_element_type=jnp.float32)
        * scaling
    )
    is_live = (jnp.arange(context)[None, :] < lengths[:, None])[:, None, None, :]
    cached = jnp.where(is_live, cached, -jnp.inf)
    peak_score = jnp.maximum(jnp.max(cached, axis=-1), own_score)
    weights = jnp.where(is_live, jnp.exp(cached - peak_score[..., None]), 0.0)
    own_weight = jnp.exp(own_score - peak_score)
    total = jnp.sum(weights, axis=-1) + own_weight
    own_prob = lax.optimization_barrier(own_weight.astype(jnp.bfloat16)).astype(jnp.float32)
    mixed = jnp.einsum(
        "rgjc,rgcd->rgjd",
        weights.astype(jnp.bfloat16),
        cached_value_rows,
        preferred_element_type=jnp.float32,
    )
    mixed = mixed + own_prob[..., None] * new_values.astype(jnp.float32).reshape(
        row_count, kv_heads, 1, head_dim
    )
    return (mixed / total[..., None]).astype(jnp.bfloat16).reshape(row_count, heads * head_dim)


def ring_order(size):
    if size == 8:
        return [0, 2, 4, 6, 7, 5, 3, 1]
    return list(range(size))


def shards(
    states, norm_gain, w_query, keyvalue_weight, w_output, key_cache, cached_value_rows, lengths
):
    size = lax.axis_size("gx")
    me = lax.axis_index("gx")
    core = lax.axis_index("gy")
    order = ring_order(size)
    order_arr = jnp.array(order, jnp.int32)
    place_arr = jnp.array([order.index(i) for i in range(size)], jnp.int32)
    place = place_arr[me]
    hops = {1: [(order[i], order[(i + 1) % size]) for i in range(size)],
            -1: [(order[(i + 1) % size], order[i]) for i in range(size)]}
    long_way = size // 2
    reach = {(1, 0): long_way, (-1, 0): size - 1 - long_way,
             (1, 1): size - 1 - long_way, (-1, 1): long_way}
    chains = list(reach)

    def at_place(offset):
        return order_arr[lax.rem(place + offset + size, size)]

    row_count, width = states.shape
    half_rows = row_count // 2
    other = 1 - core

    def half_of(array, half):
        return lax.dynamic_slice_in_dim(
            array, jnp.where(half == 0, other, core) * half_rows, half_rows, 0
        )

    state_halves = [half_of(states, 0), half_of(states, 1)]

    states_f = states.astype(jnp.float32)
    gain_all = lax.dynamic_update_slice(
        jnp.zeros((size * width,), jnp.float32), norm_gain.astype(jnp.float32), (me * width,)
    )
    both = jnp.concatenate([jnp.sum(states_f * states_f, axis=1), gain_all])
    if size & (size - 1) == 0:
        stride = 1
        while stride < size:
            both = both + lax.ppermute(both, "gx", [(i, i ^ stride) for i in range(size)])
            stride *= 2
    else:
        both = lax.psum(both, "gx")
    squares = both[:row_count]
    squares = squares + lax.ppermute(squares, "gy", [(0, 1), (1, 0)])
    output_cols = w_output.reshape(w_output.shape[0], size, w_output.shape[3])
    out_blocks, squares = lax.optimization_barrier(
        (jnp.transpose(output_cols, (1, 0, 2)), squares)
    )
    norm_scale = lax.rsqrt(squares / MODEL_WIDTH + epsilon)
    gain_mine = both[row_count:]
    scale_halves = [half_of(norm_scale, 0), half_of(norm_scale, 1)]

    def project(raw, half, owner):
        gain = lax.dynamic_slice_in_dim(gain_mine, owner * width, width, 0)
        normed = (
            raw.astype(jnp.float32) * scale_halves[half][:, None] * gain[None, :]
        ).astype(jnp.bfloat16)
        wq = lax.dynamic_slice_in_dim(w_query, owner * width, width, 0)
        wkv = lax.dynamic_slice_in_dim(keyvalue_weight, owner * width, width, 0)
        return (
            jnp.dot(normed, wq, preferred_element_type=jnp.float32),
            jnp.dot(normed, wkv, preferred_element_type=jnp.float32),
        )

    held = {chain: state_halves[chain[1]] for chain in chains}
    sums = [None, None]

    def add_to(half, pair):
        old = sums[half]
        sums[half] = pair if old is None else (old[0] + pair[0], old[1] + pair[1])

    for step in range(1, long_way + 1):
        arrived = {}
        for chain in chains:
            if step <= reach[chain]:
                arrived[chain] = lax.ppermute(held[chain], "gx", hops[chain[0]])
        if step == 1:
            for half in (0, 1):
                add_to(half, project(state_halves[half], half, me))
        for chain, raw in arrived.items():
            add_to(chain[1], project(raw, chain[1], at_place(-chain[0] * step)))
        held.update(arrived)

    joined = [jnp.concatenate([q, kv], axis=1).astype(jnp.bfloat16) for q, kv in sums]
    pair = [(0, 1), (1, 0)]
    from_other = lax.ppermute(joined[0], "gy", pair)
    mine = (joined[1].astype(jnp.float32) + from_other.astype(jnp.float32)).astype(jnp.bfloat16)

    query_width = w_query.shape[1]
    rows_here = half_rows // size
    spread = lax.all_to_all(
        mine.reshape(size, rows_here, mine.shape[1]), "gx", split_axis=0, concat_axis=0, tiled=True
    )
    spread = jnp.transpose(spread, (1, 0, 2))
    queries = spread[:, :, :query_width].reshape(rows_here, -1)
    keyvals = spread[:, :, query_width:].reshape(rows_here, -1)
    key_span_width = keyvals.shape[1] // 2
    attended = attend(
        queries,
        keyvals[:, :key_span_width],
        keyvals[:, key_span_width:],
        key_cache,
        cached_value_rows,
        lengths,
    )
    own_rows = lax.all_to_all(attended, "gx", split_axis=1, concat_axis=0, tiled=True)
    other_rows = lax.ppermute(own_rows, "gy", pair)
    head_rows = [other_rows, own_rows]

    def term(half, dest):
        block = lax.dynamic_index_in_dim(out_blocks, at_place(dest), 0, keepdims=False)
        return jnp.dot(head_rows[half], block, preferred_element_type=jnp.float32)

    moving = {}
    for step in range(long_way, 0, -1):
        for chain in chains[2:] + chains[:2]:
            if step <= reach[chain]:
                value = term(chain[1], chain[0] * step)
                if chain in moving:
                    value = value + moving[chain].astype(jnp.float32)
                moving[chain] = lax.ppermute(value.astype(jnp.bfloat16), "gx", hops[chain[0]])
    halves = []
    for half in (0, 1):
        total = state_halves[half].astype(jnp.float32) + term(half, 0)
        for chain in chains:
            if chain[1] == half and chain in moving:
                total = total + moving[chain].astype(jnp.float32)
        halves.append(total.astype(jnp.bfloat16))
    out = jnp.zeros((row_count, width), jnp.bfloat16)
    out = lax.dynamic_update_slice(out, halves[0], (other * half_rows, 0))
    return lax.dynamic_update_slice(out, halves[1], (core * half_rows, 0))


def solution(mesh):
    return jax.shard_map(
        shards,
        mesh=mesh,
        in_specs=(
            P("groups", ("gy", "gx")),
            P(("gy", "gx")),
            P("gy", "gx"),
            P("gy", "gx"),
            P("gx", "gy", None, None),
            P(("groups", "gy", "gx"), None, None, None),
            P(("groups", "gy", "gx"), None, None, None),
            P(("groups", "gy", "gx")),
        ),
        out_specs=P("groups", ("gy", "gx")),
        check_vma=False,
    )
```

```python
import math

import jax
import jax.numpy as jnp
from jax import lax
from jax.sharding import PartitionSpec as P

MODEL_WIDTH = 16384


epsilon = 1e-05
rope_base = 500000.0


def rotate(vectors, positions):
    middle = vectors.shape[-1] // 2
    frequency = rope_base ** (-jnp.arange(middle, dtype=jnp.float32) * 2.0 / vectors.shape[-1])
    angles = positions.astype(jnp.float32)[:, None] * frequency[None, :]
    cosine = jnp.cos(angles)[:, None, :]
    sine_part = jnp.sin(angles)[:, None, :]
    leading = vectors[..., :middle]
    trailing = vectors[..., middle:]
    return jnp.concatenate(
        [leading * cosine - trailing * sine_part, trailing * cosine + leading * sine_part], axis=-1
    )


def attend(queries, new_keys, new_values, key_cache, cached_value_rows, lengths):
    row_count, kv_heads, context, head_dim = key_cache.shape
    heads = queries.shape[1] // head_dim
    per_group = heads // kv_heads
    query_rot = rotate(
        queries.astype(jnp.float32).reshape(row_count, heads, head_dim), lengths
    ).astype(jnp.bfloat16)
    key_rot = rotate(
        new_keys.astype(jnp.float32).reshape(row_count, kv_heads, head_dim), lengths
    ).astype(jnp.bfloat16)
    query_grp = query_rot.reshape(row_count, kv_heads, per_group, head_dim)
    scaling = 1.0 / math.sqrt(head_dim)
    cached = (
        jnp.einsum("rgjd,rgcd->rgjc", query_grp, key_cache, preferred_element_type=jnp.float32)
        * scaling
    )
    own_score = (
        jnp.einsum("rgjd,rgd->rgj", query_grp, key_rot, preferred_element_type=jnp.float32)
        * scaling
    )
    is_live = (jnp.arange(context)[None, :] < lengths[:, None])[:, None, None, :]
    cached = jnp.where(is_live, cached, -jnp.inf)
    peak_score = jnp.maximum(jnp.max(cached, axis=-1), own_score)
    weights = jnp.where(is_live, jnp.exp(cached - peak_score[..., None]), 0.0)
    own_weight = jnp.exp(own_score - peak_score)
    total = jnp.sum(weights, axis=-1) + own_weight
    own_prob = lax.optimization_barrier(own_weight.astype(jnp.bfloat16)).astype(jnp.float32)
    mixed = jnp.einsum(
        "rgjc,rgcd->rgjd",
        weights.astype(jnp.bfloat16),
        cached_value_rows,
        preferred_element_type=jnp.float32,
    )
    mixed = mixed + own_prob[..., None] * new_values.astype(jnp.float32).reshape(
        row_count, kv_heads, 1, head_dim
    )
    return (mixed / total[..., None]).astype(jnp.bfloat16).reshape(row_count, heads * head_dim)


def ring_order(size):
    if size == 8:
        return [0, 2, 4, 6, 7, 5, 3, 1]
    return list(range(size))


def shards(
    states, norm_gain, w_query, keyvalue_weight, w_output, key_cache, cached_value_rows, lengths
):
    size = lax.axis_size("gx")
    me = lax.axis_index("gx")
    core = lax.axis_index("gy")
    order = ring_order(size)
    order_arr = jnp.array(order, jnp.int32)
    place_arr = jnp.array([order.index(i) for i in range(size)], jnp.int32)
    place = place_arr[me]
    hops = {1: [(order[i], order[(i + 1) % size]) for i in range(size)],
            -1: [(order[(i + 1) % size], order[i]) for i in range(size)]}
    long_way = size // 2
    reach = {(1, 0): long_way, (-1, 0): size - 1 - long_way,
             (1, 1): size - 1 - long_way, (-1, 1): long_way}
    chains = list(reach)

    def at_place(offset):
        return order_arr[lax.rem(place + offset + size, size)]

    row_count, width = states.shape
    half_rows = row_count // 2
    other = 1 - core

    def half_of(array, half):
        return lax.dynamic_slice_in_dim(
            array, jnp.where(half == 0, other, core) * half_rows, half_rows, 0
        )

    state_halves = [half_of(states, 0), half_of(states, 1)]

    states_f = states.astype(jnp.float32)
    gain_all = lax.dynamic_update_slice(
        jnp.zeros((size * width,), jnp.float32), norm_gain.astype(jnp.float32), (me * width,)
    )
    both = jnp.concatenate([jnp.sum(states_f * states_f, axis=1), gain_all])
    if size & (size - 1) == 0:
        stride = 1
        while stride < size:
            both = both + lax.ppermute(both, "gx", [(i, i ^ stride) for i in range(size)])
            stride *= 2
    else:
        both = lax.psum(both, "gx")
    squares = both[:row_count]
    squares = squares + lax.ppermute(squares, "gy", [(0, 1), (1, 0)])
    output_cols = w_output.reshape(w_output.shape[0], size, w_output.shape[3])
    out_blocks, squares = lax.optimization_barrier(
        (jnp.transpose(output_cols, (1, 0, 2)), squares)
    )
    norm_scale = lax.rsqrt(squares / MODEL_WIDTH + epsilon)
    gain_mine = both[row_count:]
    scale_halves = [half_of(norm_scale, 0), half_of(norm_scale, 1)]

    def project(raw, half, owner):
        gain = lax.dynamic_slice_in_dim(gain_mine, owner * width, width, 0)
        normed = (
            raw.astype(jnp.float32) * scale_halves[half][:, None] * gain[None, :]
        ).astype(jnp.bfloat16)
        wq = lax.dynamic_slice_in_dim(w_query, owner * width, width, 0)
        wkv = lax.dynamic_slice_in_dim(keyvalue_weight, owner * width, width, 0)
        return (
            jnp.dot(normed, wq, preferred_element_type=jnp.float32),
            jnp.dot(normed, wkv, preferred_element_type=jnp.float32),
        )

    held = {chain: state_halves[chain[1]] for chain in chains}
    sums = [None, None]

    def add_to(half, pair):
        old = sums[half]
        sums[half] = pair if old is None else (old[0] + pair[0], old[1] + pair[1])

    for step in range(1, long_way + 1):
        arrived = {}
        for chain in chains:
            if step <= reach[chain]:
                arrived[chain] = lax.ppermute(held[chain], "gx", hops[chain[0]])
        if step == 1:
            for half in (0, 1):
                add_to(half, project(state_halves[half], half, me))
        for chain, raw in arrived.items():
            add_to(chain[1], project(raw, chain[1], at_place(-chain[0] * step)))
        held.update(arrived)

    joined = [jnp.concatenate([q, kv], axis=1).astype(jnp.bfloat16) for q, kv in sums]
    pair = [(0, 1), (1, 0)]
    from_other = lax.ppermute(joined[0], "gy", pair)
    mine = (joined[1].astype(jnp.float32) + from_other.astype(jnp.float32)).astype(jnp.bfloat16)

    query_width = w_query.shape[1]
    rows_here = half_rows // size
    spread = lax.all_to_all(
        mine.reshape(size, rows_here, mine.shape[1]), "gx", split_axis=0, concat_axis=0, tiled=True
    )
    spread = jnp.transpose(spread, (1, 0, 2))
    queries = spread[:, :, :query_width].reshape(rows_here, -1)
    keyvals = spread[:, :, query_width:].reshape(rows_here, -1)
    key_span_width = keyvals.shape[1] // 2
    part_rows = rows_here // 2
    head_rows = []
    for part in (0, 1):
        span = slice(part * part_rows, (part + 1) * part_rows)
        attended = attend(
            queries[span],
            keyvals[span, :key_span_width],
            keyvals[span, key_span_width:],
            key_cache[span],
            cached_value_rows[span],
            lengths[span],
        )
        own_rows = lax.all_to_all(attended, "gx", split_axis=1, concat_axis=0, tiled=True)
        other_rows = lax.ppermute(own_rows, "gy", pair)
        head_rows.append(jnp.concatenate([own_rows, other_rows], axis=0))
    parted = states.reshape(2, size, 2, part_rows, width)

    def term(half, dest):
        block = lax.dynamic_index_in_dim(out_blocks, at_place(dest), 0, keepdims=False)
        return jnp.dot(head_rows[half], block, preferred_element_type=jnp.float32)

    moving = {}
    for step in range(long_way, 0, -1):
        for chain in chains:
            if step <= reach[chain]:
                value = term(chain[1], chain[0] * step)
                if chain in moving:
                    value = value + moving[chain].astype(jnp.float32)
                moving[chain] = lax.ppermute(value.astype(jnp.bfloat16), "gx", hops[chain[0]])
    halves = []
    for half in (0, 1):
        total = term(half, 0)
        for chain in chains:
            if chain[1] == half and chain in moving:
                total = total + moving[chain].astype(jnp.float32)
        total = total.reshape(2, size, part_rows, width)
        total = jnp.where(core == 0, total, total[::-1])
        halves.append((parted[:, :, half].astype(jnp.float32) + total).astype(jnp.bfloat16))
    return jnp.stack(halves, axis=2).reshape(row_count, width)


def solution(mesh):
    return jax.shard_map(
        shards,
        mesh=mesh,
        in_specs=(
            P("groups", ("gy", "gx")),
            P(("gy", "gx")),
            P("gy", "gx"),
            P("gy", "gx"),
            P("gx", "gy", None, None),
            P(("groups", "gy", "gx"), None, None, None),
            P(("groups", "gy", "gx"), None, None, None),
            P(("groups", "gy", "gx")),
        ),
        out_specs=P("groups", ("gy", "gx")),
        check_vma=False,
    )
```

```python
import math

import jax
import jax.numpy as jnp
from jax import lax
from jax.sharding import PartitionSpec as P

MODEL_WIDTH = 16384


epsilon = 1e-05
rope_base = 500000.0


def rotate(vectors, positions):
    middle = vectors.shape[-1] // 2
    frequency = rope_base ** (-jnp.arange(middle, dtype=jnp.float32) * 2.0 / vectors.shape[-1])
    angles = positions.astype(jnp.float32)[:, None] * frequency[None, :]
    cosine = jnp.cos(angles)[:, None, :]
    sine_part = jnp.sin(angles)[:, None, :]
    leading = vectors[..., :middle]
    trailing = vectors[..., middle:]
    return jnp.concatenate(
        [leading * cosine - trailing * sine_part, trailing * cosine + leading * sine_part], axis=-1
    )


def attend(queries, new_keys, new_values, key_cache, cached_value_rows, lengths):
    row_count, kv_heads, context, head_dim = key_cache.shape
    heads = queries.shape[1] // head_dim
    per_group = heads // kv_heads
    query_rot = rotate(
        queries.astype(jnp.float32).reshape(row_count, heads, head_dim), lengths
    ).astype(jnp.bfloat16)
    key_rot = rotate(
        new_keys.astype(jnp.float32).reshape(row_count, kv_heads, head_dim), lengths
    ).astype(jnp.bfloat16)
    query_grp = query_rot.reshape(row_count, kv_heads, per_group, head_dim)
    scaling = 1.0 / math.sqrt(head_dim)
    cached = (
        jnp.einsum("rgjd,rgcd->rgjc", query_grp, key_cache, preferred_element_type=jnp.float32)
        * scaling
    )
    own_score = (
        jnp.einsum("rgjd,rgd->rgj", query_grp, key_rot, preferred_element_type=jnp.float32)
        * scaling
    )
    is_live = (jnp.arange(context)[None, :] < lengths[:, None])[:, None, None, :]
    cached = jnp.where(is_live, cached, -jnp.inf)
    peak_score = jnp.maximum(jnp.max(cached, axis=-1), own_score)
    weights = jnp.where(is_live, jnp.exp(cached - peak_score[..., None]), 0.0)
    own_weight = jnp.exp(own_score - peak_score)
    total = jnp.sum(weights, axis=-1) + own_weight
    own_prob = lax.optimization_barrier(own_weight.astype(jnp.bfloat16)).astype(jnp.float32)
    mixed = jnp.einsum(
        "rgjc,rgcd->rgjd",
        weights.astype(jnp.bfloat16),
        cached_value_rows,
        preferred_element_type=jnp.float32,
    )
    mixed = mixed + own_prob[..., None] * new_values.astype(jnp.float32).reshape(
        row_count, kv_heads, 1, head_dim
    )
    return (mixed / total[..., None]).astype(jnp.bfloat16).reshape(row_count, heads * head_dim)


def ring_order(size):
    if size == 8:
        return [0, 2, 4, 6, 7, 5, 3, 1]
    return list(range(size))


def shards(
    states, norm_gain, w_query, keyvalue_weight, w_output, key_cache, cached_value_rows, lengths
):
    size = lax.axis_size("gx")
    me = lax.axis_index("gx")
    core = lax.axis_index("gy")
    order = ring_order(size)
    order_arr = jnp.array(order, jnp.int32)
    place_arr = jnp.array([order.index(i) for i in range(size)], jnp.int32)
    place = place_arr[me]
    hops = {1: [(order[i], order[(i + 1) % size]) for i in range(size)],
            -1: [(order[(i + 1) % size], order[i]) for i in range(size)]}
    long_way = size // 2
    reach = {(1, 0): long_way, (-1, 0): size - 1 - long_way,
             (1, 1): size - 1 - long_way, (-1, 1): long_way}
    chains = list(reach)

    def at_place(offset):
        return order_arr[lax.rem(place + offset + size, size)]

    row_count, width = states.shape
    half_rows = row_count // 2
    other = 1 - core

    def half_of(array, half):
        return lax.dynamic_slice_in_dim(
            array, jnp.where(half == 0, other, core) * half_rows, half_rows, 0
        )

    state_halves = [half_of(states, 0), half_of(states, 1)]

    states_f = states.astype(jnp.float32)
    gain_all = lax.dynamic_update_slice(
        jnp.zeros((size * width,), jnp.float32), norm_gain.astype(jnp.float32), (me * width,)
    )
    both = jnp.concatenate([jnp.sum(states_f * states_f, axis=1), gain_all])
    if size & (size - 1) == 0:
        stride = 1
        while stride < size:
            both = both + lax.ppermute(both, "gx", [(i, i ^ stride) for i in range(size)])
            stride *= 2
    else:
        both = lax.psum(both, "gx")
    squares = both[:row_count]
    squares = squares + lax.ppermute(squares, "gy", [(0, 1), (1, 0)])
    output_cols = w_output.reshape(w_output.shape[0], size, w_output.shape[3])
    out_blocks, squares = lax.optimization_barrier(
        (jnp.transpose(output_cols, (1, 0, 2)), squares)
    )
    norm_scale = lax.rsqrt(squares / MODEL_WIDTH + epsilon)
    gain_mine = both[row_count:]
    scale_halves = [half_of(norm_scale, 0), half_of(norm_scale, 1)]

    def project(raw, half, owner):
        gain = lax.dynamic_slice_in_dim(gain_mine, owner * width, width, 0)
        normed = (
            raw.astype(jnp.float32) * scale_halves[half][:, None] * gain[None, :]
        ).astype(jnp.bfloat16)
        wq = lax.dynamic_slice_in_dim(w_query, owner * width, width, 0)
        wkv = lax.dynamic_slice_in_dim(keyvalue_weight, owner * width, width, 0)
        return (
            jnp.dot(normed, wq, preferred_element_type=jnp.float32),
            jnp.dot(normed, wkv, preferred_element_type=jnp.float32),
        )

    held = {chain: state_halves[chain[1]] for chain in chains}
    sums = [None, None]

    def add_to(half, pair):
        old = sums[half]
        sums[half] = pair if old is None else (old[0] + pair[0], old[1] + pair[1])

    for step in range(1, long_way + 1):
        arrived = {}
        for chain in chains:
            if step <= reach[chain]:
                arrived[chain] = lax.ppermute(held[chain], "gx", hops[chain[0]])
        if step == 1:
            for half in (0, 1):
                add_to(half, project(state_halves[half], half, me))
        for chain, raw in arrived.items():
            add_to(chain[1], project(raw, chain[1], at_place(-chain[0] * step)))
        held.update(arrived)

    joined = [jnp.concatenate([q, kv], axis=1).astype(jnp.bfloat16) for q, kv in sums]
    pair = [(0, 1), (1, 0)]
    from_other = lax.ppermute(joined[0], "gy", pair)
    mine = (joined[1].astype(jnp.float32) + from_other.astype(jnp.float32)).astype(jnp.bfloat16)

    query_width = w_query.shape[1]
    rows_here = half_rows // size
    spread = lax.all_to_all(
        mine.reshape(size, rows_here, mine.shape[1]), "gx", split_axis=0, concat_axis=0, tiled=True
    )
    spread = jnp.transpose(spread, (1, 0, 2))
    queries = spread[:, :, :query_width].reshape(rows_here, -1)
    keyvals = spread[:, :, query_width:].reshape(rows_here, -1)
    key_span_width = keyvals.shape[1] // 2
    part_rows = rows_here // 2
    head_rows = []
    ready = {}

    def term(half, dest):
        block = lax.dynamic_index_in_dim(out_blocks, at_place(dest), 0, keepdims=False)
        return jnp.dot(head_rows[half], block, preferred_element_type=jnp.float32)

    for part in (0, 1):
        span = slice(part * part_rows, (part + 1) * part_rows)
        attended = attend(
            queries[span],
            keyvals[span, :key_span_width],
            keyvals[span, key_span_width:],
            key_cache[span],
            cached_value_rows[span],
            lengths[span],
        )
        if part == 1:
            for chain in chains[:2]:
                first = term(0, chain[0] * reach[chain]).astype(jnp.bfloat16)
                ready[chain], attended = lax.optimization_barrier((first, attended))
        own_rows = lax.all_to_all(attended, "gx", split_axis=1, concat_axis=0, tiled=True)
        other_rows = lax.ppermute(own_rows, "gy", pair)
        head_rows.append(jnp.concatenate([own_rows, other_rows], axis=0))
    parted = states.reshape(2, size, 2, part_rows, width)

    moving = {}
    for step in range(long_way, 0, -1):
        for chain in chains:
            if step <= reach[chain]:
                if chain in ready:
                    value = ready.pop(chain)
                else:
                    value = term(chain[1], chain[0] * step)
                if chain in moving:
                    value = value + moving[chain].astype(jnp.float32)
                moving[chain] = lax.ppermute(value.astype(jnp.bfloat16), "gx", hops[chain[0]])
    halves = []
    for half in (0, 1):
        total = term(half, 0)
        for chain in chains:
            if chain[1] == half and chain in moving:
                total = total + moving[chain].astype(jnp.float32)
        total = total.reshape(2, size, part_rows, width)
        total = jnp.where(core == 0, total, total[::-1])
        halves.append((parted[:, :, half].astype(jnp.float32) + total).astype(jnp.bfloat16))
    return jnp.stack(halves, axis=2).reshape(row_count, width)


def solution(mesh):
    return jax.shard_map(
        shards,
        mesh=mesh,
        in_specs=(
            P("groups", ("gy", "gx")),
            P(("gy", "gx")),
            P("gy", "gx"),
            P("gy", "gx"),
            P("gx", "gy", None, None),
            P(("groups", "gy", "gx"), None, None, None),
            P(("groups", "gy", "gx"), None, None, None),
            P(("groups", "gy", "gx")),
        ),
        out_specs=P("groups", ("gy", "gx")),
        check_vma=False,
    )
```
